128 devices in a mesh: blk: 16 (over z_lo, x, core), seq: 8 (over z_hi, y).
Axes of the slice: x: 4, y: 4, z: 4 (z_hi: 2, z_lo: 2; z = z_hi * 2 + z_lo), core: 2. Of those that a mesh axis runs over, the one named last changes fastest.
Arguments:
- row_inputs: bfloat16 [8192, 3072], P('blk'), may hold values from -6 to 6
- row_grads: bfloat16 [8192, 3072], P('blk'), may hold values from -3 to 3
- gate_prob: float32 [8192], P('blk'), may hold values from 0.05 to 1
- live_counts: int32 [16], P('blk'), may hold values from 1 to 512, as said below
- gate_weight: bfloat16 [3072, 8192], P(None, ('blk', 'seq')), may hold values from -0.109375 to 0.109375
- up_weight: bfloat16 [3072, 8192], P(None, ('blk', 'seq')), may hold values from -0.109375 to 0.109375
- down_weight: bfloat16 [8192, 3072], P(('blk', 'seq')), may hold values from -0.0625 to 0.0625
Outputs:
- input_grad: bfloat16 [8192, 3072], P(('blk', 'seq'))
- prob_grad: float32 [8192], P(('blk', 'seq'))
- gate_grad: bfloat16 [3072, 8192], P(None, ('blk', 'seq'))
- up_grad: bfloat16 [3072, 8192], P(None, ('blk', 'seq'))
- down_grad: bfloat16 [8192, 3072], P(('blk', 'seq'))
The draws below stay inside these ranges and needn't reach their ends.
Inputs may be any that keep to these rules, and one draw needn't show every extreme that they name: live_counts[b] routed rows fill the first slots of group b; the others are padding; in every draw some group is full.
All inputs are finite; a program needn't handle non-finite values.
Results may differ from the reference program's by a relative error of at most 0.023.
Values may be sent and summed in bfloat16 or wider, within the bound.
A program may use at most 192 MiB of HBM per device.

```python
import jax
import jax.numpy as jnp
from jax import lax

D = 3072
FF = 8192
ROWS_DEV = 512
GROUPS = 16
SHARES = 8
UNITS = 64
ROWS = 8192


def draw_live_counts(key, part):
    key = jax.random.fold_in(key, 11)
    spread_key, chosen_key = jax.random.split(key)
    counts = jax.random.randint(spread_key, (GROUPS,), 1, ROWS_DEV + 1)
    fullest = jax.random.randint(chosen_key, (), 0, GROUPS)
    return jnp.where(jnp.arange(GROUPS) == fullest, ROWS_DEV, counts).astype(jnp.int32)


def steps_of(rng, dims, shards, least, high):
    gain = 1.0
    for dim, shards_of in shards:
        steps = jax.random.uniform(jax.random.fold_in(jax.random.fold_in(rng, 6), dim), (shards_of,), jnp.float32, least / len(shards), high / len(shards))
        gain = gain * jnp.repeat(jnp.exp(steps), dims[dim] // shards_of).reshape((-1,) + (1,) * (len(dims) - 1 - dim))
    return gain


def scatter_about(rng, shape, spread, limit, cuts=(), kind=jnp.bfloat16):
    loudness = steps_of(rng, shape, cuts, -0.22, 0.18) if cuts else 1.0
    array = jax.random.normal(rng, shape, jnp.float32) * spread * loudness
    return jnp.minimum(jnp.maximum(array, -limit), limit).astype(kind)


def setup_inputs(seed: int = 0) -> dict:
    arg_keys = jax.random.split(jax.random.key(seed), 8)
    row_inputs = scatter_about(arg_keys[0], (ROWS, D), 1.0, 6.0, ((0, 16),))
    row_grads = scatter_about(arg_keys[1], (ROWS, D), 0.5, 3.0, ((0, 16),))
    gate_prob = jnp.clip(0.05 + 0.95 * jax.random.uniform(arg_keys[2], (ROWS,), jnp.float32) ** steps_of(arg_keys[2], (ROWS,), ((0, 16),), -0.2, 0.2), 0.05, 1.0)
    live_counts = draw_live_counts(jax.random.fold_in(arg_keys[7], 71), 0)
    gate_weight = scatter_about(arg_keys[4], (D, FF), D ** -0.5, 0.109375, ((1, 128),))
    up_weight = scatter_about(arg_keys[5], (D, FF), D ** -0.5, 0.109375, ((1, 128),))
    down_weight = scatter_about(arg_keys[6], (FF, D), FF ** -0.5, 0.0625, ((0, 128),))
    return dict(row_inputs=row_inputs, row_grads=row_grads, gate_prob=gate_prob, live_counts=live_counts, gate_weight=gate_weight, up_weight=up_weight, down_weight=down_weight)


def rounded(value):
    return lax.optimization_barrier(value.astype(jnp.bfloat16)).astype(jnp.float32)


def reference(row_inputs, row_grads, gate_prob, live_counts, gate_weight, up_weight, down_weight):
    gate_shares = gate_weight.astype(jnp.float32).reshape(D, GROUPS, SHARES, UNITS)
    up_shares = up_weight.astype(jnp.float32).reshape(D, GROUPS, SHARES, UNITS)

    def one_group(totals, group_index):
        start = (group_index * ROWS_DEV).astype(jnp.int32)
        inputs_here = lax.dynamic_slice_in_dim(row_inputs, start, ROWS_DEV, 0)
        grads_here = lax.dynamic_slice_in_dim(row_grads, start, ROWS_DEV, 0)
        prob_here = lax.dynamic_slice_in_dim(gate_prob, start, ROWS_DEV, 0)
        live_mask = (jnp.arange(ROWS_DEV, dtype=jnp.int32) < live_counts[group_index]).astype(jnp.float32)
        weight_rows = live_mask * prob_here
        gate_pre = jnp.dot(inputs_here, gate_weight, preferred_element_type=jnp.float32)
        up_pre = jnp.dot(inputs_here, up_weight, preferred_element_type=jnp.float32)
        sigmoid_gate = jax.nn.sigmoid(gate_pre)
        activated = gate_pre * sigmoid_gate
        hidden = (activated * up_pre).astype(jnp.bfloat16)
        back_hidden = jnp.dot(grads_here, down_weight.T, preferred_element_type=jnp.float32)
        scaled_grads = (weight_rows[:, None] * grads_here.astype(jnp.float32)).astype(jnp.bfloat16)
        weighted_back = weight_rows[:, None] * back_hidden
        gate_back = (weighted_back * up_pre * sigmoid_gate * (1.0 + gate_pre * (1.0 - sigmoid_gate))).astype(jnp.bfloat16)
        up_back = (weighted_back * activated).astype(jnp.bfloat16)
        down_term = rounded(jnp.dot(hidden.T, scaled_grads, preferred_element_type=jnp.float32))
        gate_term = rounded(jnp.dot(inputs_here.T, gate_back, preferred_element_type=jnp.float32))
        up_term = rounded(jnp.dot(inputs_here.T, up_back, preferred_element_type=jnp.float32))
        gate_split = gate_back.astype(jnp.float32).reshape(ROWS_DEV, GROUPS, SHARES, UNITS)
        up_split = up_back.astype(jnp.float32).reshape(ROWS_DEV, GROUPS, SHARES, UNITS)
        parts = jnp.einsum("rgsu,dgsu->rsd", gate_split, gate_shares) + jnp.einsum("rgsu,dgsu->rsd", up_split, up_shares)
        input_rows = jnp.sum(rounded(parts), axis=1).astype(jnp.bfloat16)
        prob_terms = (live_mask[:, None] * hidden.astype(jnp.float32) * back_hidden).reshape(ROWS_DEV, GROUPS, SHARES, UNITS)
        prob_rows = jnp.sum(rounded(jnp.sum(prob_terms, axis=(1, 3))), axis=1)
        new_totals = (totals[0] + gate_term, totals[1] + up_term, totals[2] + down_term)
        return new_totals, (input_rows, prob_rows)

    start_totals = (jnp.zeros((D, FF), jnp.float32), jnp.zeros((D, FF), jnp.float32), jnp.zeros((FF, D), jnp.float32))
    totals, outputs = lax.scan(one_group, start_totals, jnp.arange(GROUPS, dtype=jnp.int32))
    input_grad = outputs[0].reshape(ROWS, D)
    prob_grad = outputs[1].reshape(ROWS)
    return (input_grad, prob_grad, totals[0].astype(jnp.bfloat16), totals[1].astype(jnp.bfloat16), totals[2].astype(jnp.bfloat16))
```

```python
import functools

import jax
import jax.numpy as jnp
from jax import lax
from jax.experimental import pallas as pl
from jax.experimental.pallas import tpu as pltpu
from jax.sharding import PartitionSpec as P

MESH = pl.DeviceIdType.MESH
BF16 = jnp.bfloat16
F32 = jnp.float32
NT = (((1,), (1,)), ((), ()))
NN = (((1,), (0,)), ((), ()))

L0, Z0 = (0, 0), (0, 1)
L2, Z2 = (3, 0), (3, 1)
CHUNKS = (0, 1, 2)
ALONG_X = (0, 2)


def l_at(step):
    return (1, (1 - step) // 2)


def z_at(step):
    return (2, (1 - step) // 2)


def kernel(
    x_hbm, g_hbm, wc_hbm, gate_hbm, up_hbm, down_hbm,
    gu_out, down_out, in_out, prob_out,
    X, G, WC, W, GB, AT, PT, DG, RZ, RZX, RX2, RXF, IG, SIB, YR2, YF, ZF, LH,
    PB, SIBP, PR2, PF, PZ,
    local_sem, send_sem, recv_sem,
    *, units, rows, feats, blocks,
):
    U = units
    rb, nb_dw, nb_ig = blocks
    part = rows // 8
    blk, seq = lax.axis_index("blk"), lax.axis_index("seq")
    c = lax.rem(blk, 2)
    x = lax.rem(blk // 2, 4)
    y = lax.rem(seq, 4)
    zh = seq // 4
    z = zh * 2 + blk // 8
    up = 1 - 2 * c

    def device(xx, yy, zz, cc):
        xx, yy, zz = lax.rem(xx + 8, 4), lax.rem(yy + 8, 4), lax.rem(zz + 8, 4)
        return ((lax.rem(zz, 2) * 4 + xx) * 2 + cc, (zz // 2) * 4 + yy)

    def along_x(step):
        return device(x + step, y, z, c)

    def along_y(step):
        return device(x, y + step, z, c)

    z_next, z_back, z_far = device(x, y, z + up, c), device(x, y, z - up, c), device(x, y, z + 2, c)
    sibling = device(x, y, z, 1 - c)
    turn = (1, up, -1)

    def chunk(ref, slot, j):
        pair, half = slot
        start = j * 2 * U + half * U
        if not isinstance(start, int):
            start = pl.multiple_of(start, U)
        return ref.at[pair, pl.ds(start, U), :]

    pending = []
    used = [0]

    def ids(count):
        used[0] += count
        return used[0] - count

    def transfer(src, dst, number, target):
        return pltpu.make_async_remote_copy(
            src_ref=src, dst_ref=dst, send_sem=send_sem.at[number], recv_sem=recv_sem.at[number],
            device_id=target, device_id_type=MESH,
        )

    def start(copy):
        copy.start()
        pending.append(copy)
        return copy

    n_l = ids(6)
    n_z0 = ids(3)
    n_l2 = ids(3)
    n_z = ids(6)
    n_z2 = ids(3)
    n_rz = ids(12)
    n_rzx = ids(3)
    n_rx2 = ids(3)
    n_rxf = ids(6)
    n_row = ids(3)
    n_sib = ids(2)
    n_sibp = ids(1)
    n_y2 = ids(4)
    n_yf = ids(4)
    n_yfp = ids(4)
    n_zf = ids(2)

    def side(step):
        return (1 - step) // 2

    own = (gate_hbm, up_hbm, down_hbm)

    def send_l(step, j):
        return transfer(own[j], chunk(W, l_at(-step), j), n_l + side(-step) * 3 + j, along_x(step))

    def send_z0(j):
        return transfer(own[j], chunk(W, Z0, j), n_z0 + j, z_next)

    def send_l2(j):
        return transfer(chunk(W, l_at(-turn[j]), j), chunk(W, L2, j), n_l2 + j, along_x(turn[j]))

    def send_z(step, j):
        return transfer(chunk(W, l_at(step), j), chunk(W, z_at(step), j), n_z + side(step) * 3 + j, z_next)

    def send_z2(j):
        if j in ALONG_X:
            return transfer(chunk(W, z_at(-turn[j]), j), chunk(W, Z2, j), n_z2 + j, along_x(turn[j]))
        return transfer(chunk(W, L2, j), chunk(W, Z2, j), n_z2 + j, z_next)

    def back_z(slot, which, j):
        return transfer(chunk(DG, slot, j), RZ.at[which, j], n_rz + which * 3 + j, z_back)

    def back_z2(j):
        return transfer(chunk(DG, Z2, j), RZX.at[j // 2], n_rzx + j, along_x(turn[j]))

    def back_l2(j):
        return transfer(chunk(DG, L2, j), RX2.at[j], n_rx2 + j, along_x(turn[j]))

    def back_l(step, j):
        return transfer(
            chunk(DG, l_at(step), j), RXF.at[side(step), j], n_rxf + side(step) * 3 + j, along_x(step)
        )

    def add_to(slot, j, *terms):
        ref = chunk(DG, slot, j)
        total = ref[...].astype(F32)
        for term in terms:
            total += term[...].astype(F32)
        ref[...] = total.astype(BF16)

    def forward(p, order):
        for first in order:
            here = pl.ds(pl.multiple_of(first, rb), rb)
            pre = lax.dot_general(X[here, :], W[p, 0 : 4 * U, :], NT, preferred_element_type=F32)
            back = lax.dot_general(G[here, :], W[p, 4 * U : 6 * U, :], NT, preferred_element_type=F32)
            gate_pre, up_pre = pre[:, : 2 * U], pre[:, 2 * U :]
            s = jax.nn.sigmoid(gate_pre)
            activated = gate_pre * s
            hidden = activated * up_pre
            product = hidden.astype(BF16).astype(F32) * back
            if p == 0:
                PT[here, :] = product
            else:
                PT[here, :] += product
            weight = WC[here, :]
            weighted = weight * back
            gate_back = weighted * up_pre * s * (1.0 + gate_pre * (1.0 - s))
            up_back = weighted * activated
            GB[p, here, 0 : 2 * U] = gate_back.astype(BF16)
            GB[p, here, 2 * U :] = up_back.astype(BF16)
            AT[:, here] = jnp.concatenate([gate_back, up_back, weight * hidden], axis=1).T.astype(BF16)

    def weight_terms(p):
        def body(i, carry):
            cols = pl.ds(pl.multiple_of(i * nb_dw, nb_dw), nb_dw)
            DG[p, 0 : 4 * U, cols] = lax.dot_general(
                AT[0 : 4 * U, :], X[:, cols], NN, preferred_element_type=F32
            ).astype(BF16)
            DG[p, 4 * U :, cols] = lax.dot_general(
                AT[4 * U :, :], G[:, cols], NN, preferred_element_type=F32
            ).astype(BF16)
            return carry

        lax.fori_loop(0, feats // nb_dw, body, 0)

    steps_y = (2, 1, -1, 0)

    def row_start(group, k, h):
        return pl.multiple_of(group * rows + (h * 4 + lax.rem(y + steps_y[k] + 4, 4)) * part, part)

    def row_terms(which, group, k0):
        for i in range(4):
            here = pl.ds(row_start(group, k0 + i // 2, i % 2), part)
            for p in range(4):
                LH[i * part : (i + 1) * part, p * 4 * U : (p + 1) * 4 * U] = GB[p, here, :]

        def body(n, carry):
            cols = pl.ds(pl.multiple_of(n * nb_ig, nb_ig), nb_ig)
            total = lax.dot_general(LH[:, 0 : 4 * U], W[0, 0 : 4 * U, cols], NN, preferred_element_type=F32)
            for p in range(1, 4):
                total += lax.dot_general(
                    LH[:, p * 4 * U : (p + 1) * 4 * U], W[p, 0 : 4 * U, cols], NN, preferred_element_type=F32
                )
            for i in range(4):
                IG[which, k0 + i // 2, i % 2, :, cols] = total[i * part : (i + 1) * part].astype(BF16)
            return carry

        lax.fori_loop(0, feats // nb_ig, body, 0)

    def prob_terms():
        ones = jnp.ones((8, 2 * U), F32)
        for which in range(2):
            group = c if which == 0 else 1 - c
            for k in range(4):
                for h in range(2):
                    here = pl.ds(row_start(group, k, h), part)
                    PB[which, k, h, :, 0:part] = lax.dot_general(
                        ones, PT[here, :], NT, preferred_element_type=F32, precision=lax.Precision.HIGHEST
                    )

    mine = pl.ds(pl.multiple_of(c * rows, rows), rows)
    locals_ = [
        pltpu.make_async_copy(own[j], chunk(W, L0, j), local_sem.at[j]) for j in CHUNKS
    ] + [
        pltpu.make_async_copy(x_hbm, X.at[mine, :], local_sem.at[3]),
        pltpu.make_async_copy(g_hbm, G.at[mine, :], local_sem.at[4]),
        pltpu.make_async_copy(wc_hbm, WC.at[mine, :], local_sem.at[5]),
    ]

    barrier = pltpu.get_barrier_semaphore()
    friends = (
        along_x(1), along_x(-1), along_y(1), along_y(-1), z_next, z_back, z_far, sibling,
    )
    for friend in friends:
        pl.semaphore_signal(barrier, inc=1, device_id=friend, device_id_type=MESH)
    for copy in locals_:
        copy.start()
    PB[...] = jnp.zeros_like(PB)
    pl.semaphore_wait(barrier, len(friends))

    for j in CHUNKS:
        for step in (1, -1):
            start(send_l(step, j))
        start(send_z0(j))
    row_copies = [
        start(transfer(x_hbm, X.at[mine, :], n_row, sibling)),
        start(transfer(g_hbm, G.at[mine, :], n_row + 1, sibling)),
        start(transfer(wc_hbm, WC.at[mine, :], n_row + 2, sibling)),
    ]

    def pass_l(j):
        for step in (1, -1):
            send_l(-step, j).wait_recv()
            start(send_z(step, j))
        start(send_l2(j))

    def pass_z(j):
        for step in (1, -1):
            send_z(step, j).wait_recv()
        if j in ALONG_X:
            start(send_z2(j))

    def pass_l2(j):
        send_l2(j).wait_recv()
        if j not in ALONG_X:
            start(send_z2(j))

    own_first, other_first = c * rows, (1 - c) * rows
    pass_l(0)
    for copy in locals_:
        copy.wait()
    for j in CHUNKS:
        send_z0(j).wait_recv()
    forward(0, [own_first])
    pass_l(1)
    for copy in row_copies:
        copy.wait_recv()
    forward(0, [other_first])
    weight_terms(0)
    pass_l(2)
    pass_z(0)
    forward(1, [0, rows])
    pass_l2(0)
    pass_z(1)
    pass_l2(1)
    weight_terms(1)
    pass_l2(2)
    pass_z(2)
    forward(2, [0, rows])
    weight_terms(2)
    for j in ALONG_X:
        start(back_z(z_at(-turn[j]), 1 + side(-turn[j]), j))
    for step in (1, -1):
        start(back_z(z_at(step), 1 + side(step), 1))
    for j in CHUNKS:
        send_z2(j).wait_recv()
    forward(3, [0, rows])
    weight_terms(3)
    for j in ALONG_X:
        start(back_z2(j))
        start(back_l2(j))
    start(back_z(Z2, 3, 1))

    sib_copies = []
    row_terms(1, 1 - c, 0)
    sib_copies.append(start(transfer(IG.at[1, 0:2], SIB.at[0:2], n_sib, sibling)))
    prob_terms()
    sib_p = start(transfer(PB.at[1], SIBP, n_sibp, sibling))
    row_terms(1, 1 - c, 2)
    sib_copies.append(start(transfer(IG.at[1, 2:4], SIB.at[2:4], n_sib + 1, sibling)))
    for j in ALONG_X:
        back_z2(j).wait_recv()
        add_to(z_at(turn[j]), j, RZX.at[j // 2])
        start(back_z(z_at(turn[j]), 1 + side(turn[j]), j))
    for j in CHUNKS:
        start(back_z(Z0, 0, j))
    row_terms(0, c, 0)
    for j in ALONG_X:
        back_z(z_at(-turn[j]), 1 + side(-turn[j]), j).wait_recv()
        add_to(l_at(-turn[j]), j, RZ.at[1 + side(-turn[j]), j])
        start(back_l(-turn[j], j))
    row_terms(0, c, 2)

    def add_sib(k):
        IG[0, k] = (IG[0, k].astype(F32) + SIB[k].astype(F32)).astype(BF16)

    def add_row(k, h, ref):
        IG[0, k, h] = (IG[0, k, h].astype(F32) + ref[...].astype(F32)).astype(BF16)

    def y_far(h):
        step = 1 - 2 * h
        return (
            transfer(IG.at[0, 0, h], YR2.at[h], n_y2 + h, along_y(step)),
            transfer(PB.at[0, 0, h], PR2.at[h], n_y2 + 2 + h, along_y(step)),
        )

    def y_last(k, h):
        step = steps_y[k]
        return (
            transfer(IG.at[0, k, h], YF.at[k - 1, h], n_yf + (k - 1) * 2 + h, along_y(step)),
            transfer(PB.at[0, k, h], PF.at[k - 1, h], n_yfp + (k - 1) * 2 + h, along_y(step)),
        )

    sib_copies[0].wait_recv()
    sib_p.wait_recv()
    PB[0] = PB[0] + SIBP[...]
    add_sib(0)
    for h in range(2):
        for copy in y_far(h):
            start(copy)
    add_sib(1)
    for copy in y_last(1, 1):
        start(copy)
    sib_copies[1].wait_recv()
    add_sib(2)
    for copy in y_last(2, 0):
        start(copy)
    add_sib(3)

    for step in (1, -1):
        back_z(z_at(step), 1 + side(step), 1).wait_recv()
        add_to(l_at(step), 1, RZ.at[1 + side(step), 1])
    start(back_l(-turn[1], 1))
    back_z(Z2, 3, 1).wait_recv()
    add_to(L2, 1, RZ.at[3, 1])
    start(back_l2(1))
    for j in ALONG_X:
        back_z(z_at(turn[j]), 1 + side(turn[j]), j).wait_recv()
        back_l2(j).wait_recv()
        add_to(l_at(turn[j]), j, RZ.at[1 + side(turn[j]), j], RX2.at[j])
        start(back_l(turn[j], j))
    for k, h in ((1, 0), (2, 1)):
        for copy in y_far(h):
            copy.wait_recv()
        add_row(k, h, YR2.at[h])
        PB[0, k, h] = PB[0, k, h] + PR2[h]
        for copy in y_last(k, h):
            start(copy)
    back_l2(1).wait_recv()
    add_to(l_at(turn[1]), 1, RX2.at[1])
    start(back_l(turn[1], 1))
    for k in (1, 2):
        for h in range(2):
            for copy in y_last(k, h):
                copy.wait_recv()
    IG[0, 3] = (IG[0, 3].astype(F32) + YF[0].astype(F32) + YF[1].astype(F32)).astype(BF16)
    PB[0, 3] = PB[0, 3] + PF[0] + PF[1]
    z_copies = (
        start(transfer(IG.at[0, 3, 1 - zh], ZF, n_zf, z_far)),
        start(transfer(PB.at[0, 3, 1 - zh], PZ, n_zf + 1, z_far)),
    )
    for j in CHUNKS:
        back_z(Z0, 0, j).wait_recv()
        for step in (1, -1):
            back_l(step, j).wait_recv()
        total = chunk(DG, L0, j)[...].astype(F32) + RZ[0, j].astype(F32)
        total += RXF[0, j].astype(F32) + RXF[1, j].astype(F32)
        if j < 2:
            gu_out[j * U : (j + 1) * U, :] = total.astype(BF16)
        else:
            down_out[...] = total.astype(BF16)
    for copy in z_copies:
        copy.wait_recv()
    in_out[...] = (IG[0, 3, zh].astype(F32) + ZF[...].astype(F32)).astype(BF16)
    prob_out[...] = PB[0, 3, zh] + PZ[...]
    for copy in pending:
        copy.wait_send()


N_SEMS = 65


def exchange(row_inputs, row_grads, weight_cols, gate_t, up_t, down, blocks):
    rows, feats = row_inputs.shape
    units = down.shape[0]
    part = rows // 8
    any_space = pl.BlockSpec(memory_space=pl.ANY)
    vmem = pl.BlockSpec(memory_space=pltpu.VMEM)
    piece = (units, feats)
    slab = (part, feats)
    tile = (8, 128)

    def held(*shape, kind=BF16):
        return pltpu.VMEM(shape, kind)

    return pl.pallas_call(
        functools.partial(kernel, units=units, rows=rows, feats=feats, blocks=blocks),
        out_shape=(
            jax.ShapeDtypeStruct((2 * units, feats), BF16),
            jax.ShapeDtypeStruct(piece, BF16),
            jax.ShapeDtypeStruct(slab, BF16),
            jax.ShapeDtypeStruct(tile, F32),
        ),
        in_specs=[any_space] * 6,
        out_specs=(vmem,) * 4,
        scratch_shapes=[
            held(2 * rows, feats),
            held(2 * rows, feats),
            held(2 * rows, 128, kind=F32),
            held(4, 6 * units, feats),
            held(4, 2 * rows, 4 * units),
            held(6 * units, 2 * rows),
            held(2 * rows, 2 * units, kind=F32),
            held(4, 6 * units, feats),
            held(4, 3, *piece),
            held(2, *piece),
            held(3, *piece),
            held(2, 3, *piece),
            held(2, 4, 2, *slab),
            held(4, 2, *slab),
            held(2, *slab),
            held(2, 2, *slab),
            held(*slab),
            held(4 * part, 16 * units),
            held(2, 4, 2, *tile, kind=F32),
            held(4, 2, *tile, kind=F32),
            held(2, *tile, kind=F32),
            held(2, 2, *tile, kind=F32),
            held(*tile, kind=F32),
            pltpu.SemaphoreType.DMA((6,)),
            pltpu.SemaphoreType.DMA((N_SEMS,)),
            pltpu.SemaphoreType.DMA((N_SEMS,)),
        ],
        compiler_params=pltpu.CompilerParams(
            collective_id=0, has_side_effects=True, vmem_limit_bytes=63 << 20
        ),
        cost_estimate=pl.CostEstimate(
            flops=16 * 2 * rows * 8 * units * feats, bytes_accessed=24 * rows * feats, transcendentals=16 * rows * units
        ),
        name="exchange",
    )(row_inputs, row_grads, weight_cols, gate_t, up_t, down)


def shards(blocks, row_inputs, row_grads, gate_prob, live_counts, gate_weight, up_weight, down_weight):
    rows = row_inputs.shape[0]
    units = down_weight.shape[0]
    part = rows // 8
    live = jnp.arange(rows, dtype=jnp.int32) < live_counts[0]
    weight_rows = jnp.where(live, gate_prob, 0.0)
    weight_cols = jnp.broadcast_to(weight_rows[:, None], (rows, 128))
    gu, down_grad, input_grad, prob = exchange(
        row_inputs, row_grads, weight_cols, gate_weight.T, up_weight.T, down_weight, blocks
    )
    first = lax.axis_index("seq") * part
    here = first + jnp.arange(part, dtype=jnp.int32)
    prob_grad = jnp.where(here < live_counts[0], prob[0, :part], 0.0)
    return (input_grad, prob_grad, gu[:units].T, gu[units:].T, down_grad)


def solution(mesh, blocks=(512, 1024, 1024)):
    return jax.shard_map(
        functools.partial(shards, blocks),
        mesh=mesh,
        in_specs=(
            P("blk", None),
            P("blk", None),
            P("blk"),
            P("blk"),
            P(None, ("blk", "seq")),
            P(None, ("blk", "seq")),
            P(("blk", "seq"), None),
        ),
        out_specs=(
            P(("blk", "seq"), None),
            P(("blk", "seq")),
            P(None, ("blk", "seq")),
            P(None, ("blk", "seq")),
            P(("blk", "seq"), None),
        ),
        check_vma=False,
    )
```

```python
import functools

import jax
import jax.numpy as jnp
from jax import lax
from jax.experimental import pallas as pl
from jax.experimental.pallas import tpu as pltpu
from jax.sharding import PartitionSpec as P

MESH = pl.DeviceIdType.MESH
BF16 = jnp.bfloat16
F32 = jnp.float32
NT = (((1,), (1,)), ((), ()))
NN = (((1,), (0,)), ((), ()))

(
    GO_L, GO_Z0, GO_Z, GO_L2, GO_Z2, BACK_Z0, BACK_Z, BACK_Z2, BACK_X2, BACK_L2, BACK_L,
    ROWS_X, ROWS_G, ROWS_W, TWIN, ALONG_Y, FAR_Z, PROB,
) = range(18)

L0, Z0 = (0, 0), (0, 1)
L2, Z2 = (3, 0), (3, 1)
CHUNKS = range(6)
TURN = (1, 1, 1, -1, -1, -1)
ALONG_X = (0, 1, 4, 5)
ORDER = (
    63, 61, 45, 48, 15, 46, 60, 1, 90, 64, 3, 62, 76, 18, 31, 47, 49, 33, 16, 2, 4, 19, 77, 65, 78, 6, 50, 80, 34,
    21, 35, 32, 81, 5, 66, 79, 17, 95, 96, 98, 0, 75, 30, 20, 97, 100, 99, 51, 101, 23, 102, 53, 36, 91, 55, 92, 68,
    93, 94, 52, 54, 24, 104, 103, 69, 106, 71, 115, 38, 70, 105, 26, 107, 67, 108, 25, 116, 41, 118, 56, 8, 109, 86,
    85, 111, 112, 117, 132, 124, 40, 42, 10, 110, 131, 125, 119, 27, 113, 22, 72, 120, 82, 57, 122, 133, 114, 83, 9,
    11, 28, 121, 134, 58, 127, 128, 37, 136, 12, 43, 123, 129, 135, 73, 84, 39, 87, 13, 7, 126, 29, 137, 59, 88,
    130, 74, 44, 14, 89, 138,
)


def l_at(step):
    return (1, (1 - step) // 2)


def z_at(step):
    return (2, (1 - step) // 2)


def kernel(
    x_hbm, g_hbm, prob_hbm, count_hbm, gate_hbm, up_hbm, down_hbm,
    gate_out, up_out, down_out, in_out, prob_out,
    X, G, WC, W, GB, AT, PT, DG, RZ, RZX, RX2, RXF, IG, SIB, YR2, YF, ZF, LH,
    PB, SIBP, PR2, PF, PZ, PV, count_ref,
    local_sem, send_sem, recv_sem,
    *, units, rows, feats, blocks,
):
    U = units
    nb_dw, nb_ig = blocks
    part = rows // 8
    blk, seq = lax.axis_index("blk"), lax.axis_index("seq")
    c = lax.rem(blk, 2)
    x = lax.rem(blk // 2, 4)
    y = lax.rem(seq, 4)
    zh = seq // 4
    z = zh * 2 + blk // 8
    up = 1 - 2 * c

    def device(xx, yy, zz, cc):
        xx, yy, zz = lax.rem(xx + 8, 4), lax.rem(yy + 8, 4), lax.rem(zz + 8, 4)
        return ((lax.rem(zz, 2) * 4 + xx) * 2 + cc, (zz // 2) * 4 + yy)

    def along_x(step):
        return device(x + step, y, z, c)

    def along_y(step):
        return device(x, y + step, z, c)

    z_next, z_back, z_far = device(x, y, z + up, c), device(x, y, z - up, c), device(x, y, z + 2, c)
    sibling = device(x, y, z, 1 - c)
    half = U // 2

    def chunk(ref, slot, h):
        pair, place = slot
        return ref.at[pair, pl.ds(h // 2 * 2 * U + place * U + h % 2 * half, half), :]

    def side(step):
        return (1 - step) // 2

    routes = {}
    pending = []
    here = set()

    def route(name, src, dst, target):
        number = len(routes)
        routes[name] = lambda: pltpu.make_async_remote_copy(
            src_ref=src, dst_ref=dst, send_sem=send_sem.at[number], recv_sem=recv_sem.at[number],
            device_id=target, device_id_type=MESH,
        )

    def send(*names):
        for name in names:
            copy = routes[name]()
            copy.start()
            pending.append(copy)

    def need(*names):
        for name in names:
            if name not in here:
                here.add(name)
                routes[name]().wait_recv()

    for h in CHUNKS:
        t = TURN[h]
        own = (gate_hbm, up_hbm, down_hbm)[h // 2].at[pl.ds(h % 2 * half, half), :]
        route((GO_Z0, h), own, chunk(W, Z0, h), z_next)
        route((BACK_Z0, h), chunk(DG, Z0, h), RZ.at[0, h], z_back)
        for e in (1, -1):
            route((GO_L, e, h), own, chunk(W, l_at(e), h), along_x(-e))
            route((GO_Z, e, h), chunk(W, l_at(e), h), chunk(W, z_at(e), h), z_next)
            route((BACK_Z, e, h), chunk(DG, z_at(e), h), RZ.at[1 + side(e), h], z_back)
            route((BACK_L, e, h), chunk(DG, l_at(e), h), RXF.at[side(e), h], along_x(e))
        route((GO_L2, h), chunk(W, l_at(-t), h), chunk(W, L2, h), along_x(t))
        route((BACK_L2, h), chunk(DG, L2, h), RX2.at[h], along_x(t))
        if h in ALONG_X:
            route((GO_Z2, h), chunk(W, z_at(-t), h), chunk(W, Z2, h), along_x(t))
            route((BACK_X2, h), chunk(DG, Z2, h), RZX.at[ALONG_X.index(h)], along_x(t))
        else:
            route((GO_Z2, h), chunk(W, L2, h), chunk(W, Z2, h), z_next)
            route((BACK_Z2, h), chunk(DG, Z2, h), RZ.at[3, h], z_back)

    mine = pl.ds(pl.multiple_of(c * rows, rows), rows)
    route(ROWS_X, x_hbm, X.at[mine, :], sibling)
    route(ROWS_G, g_hbm, G.at[mine, :], sibling)
    route(ROWS_W, WC.at[mine, :], WC.at[mine, :], sibling)
    for k in range(4):
        route((TWIN, k), IG.at[1, k], SIB.at[k], sibling)
    route((TWIN, PROB), PB.at[1], SIBP, sibling)

    def halves(ref):
        return [ref.at[pl.ds(q * (part // 2), part // 2), :] for q in range(2)]

    for k, h in ((0, 0), (0, 1), (1, 0), (1, 1), (2, 0), (2, 1)):
        step = (1 if h == 0 else -1) if k == 0 else (1 if k == 1 else -1)
        dst, dst_p = (YR2.at[h], PR2.at[h]) if k == 0 else (YF.at[k - 1, h], PF.at[k - 1, h])
        for q, (a, b) in enumerate(zip(halves(IG.at[0, k, h]), halves(dst))):
            route((ALONG_Y, k, h, q), a, b, along_y(step))
        route((ALONG_Y, k, h, PROB), PB.at[0, k, h], dst_p, along_y(step))
    for q, (a, b) in enumerate(zip(halves(IG.at[0, 3, 1 - zh]), halves(ZF))):
        route((FAR_Z, q), a, b, z_far)
    route((FAR_Z, PROB), PB.at[0, 3, 1 - zh], PZ, z_far)
    assert len(routes) == send_sem.shape[0]

    def add_into(out, ref, *terms):
        total = ref[...].astype(F32)
        for term in terms:
            total += term[...].astype(F32)
        out[...] = total.astype(BF16)

    def add_to(ref, *terms):
        add_into(ref, ref, *terms)

    counted = set()

    def forward(p, which, first):
        lines = pl.ds(pl.multiple_of(first, rows), rows)
        pre = lax.dot_general(X[lines, :], W[p, 0 : 4 * U, :], NT, preferred_element_type=F32)
        back = lax.dot_general(G[lines, :], W[p, 4 * U : 6 * U, :], NT, preferred_element_type=F32)
        gate_pre, up_pre = pre[:, : 2 * U], pre[:, 2 * U :]
        s = jax.nn.sigmoid(gate_pre)
        activated = gate_pre * s
        hidden = activated * up_pre
        product = hidden.astype(BF16).astype(F32) * back
        if which in counted:
            PT[lines, :] += product
        else:
            PT[lines, :] = product
        counted.add(which)
        weight = WC[lines, :]
        weighted = weight * back
        gate_back = weighted * up_pre * s * (1.0 + gate_pre * (1.0 - s))
        up_back = weighted * activated
        GB[p, lines, 0 : 2 * U] = gate_back.astype(BF16)
        GB[p, lines, 2 * U :] = up_back.astype(BF16)
        AT[:, lines] = jnp.concatenate([gate_back, up_back, weight * hidden], axis=1).T.astype(BF16)

    def weight_terms(p, first, last, rows_ref):
        def body(i, carry):
            cols = pl.ds(pl.multiple_of(i * nb_dw, nb_dw), nb_dw)
            DG[p, first:last, cols] = lax.dot_general(
                AT[first:last, :], rows_ref[:, cols], NN, preferred_element_type=F32
            ).astype(BF16)
            return carry

        lax.fori_loop(0, feats // nb_dw, body, 0)

    steps_y = (2, 1, -1, 0)

    def row_start(group, k, h):
        return pl.multiple_of(group * rows + (h * 4 + lax.rem(y + steps_y[k] + 4, 4)) * part, part)

    def row_terms(which, group, k0, pairs):
        for i in range(4):
            here = pl.ds(row_start(group, k0 + i // 2, i % 2), part)
            for n, p in enumerate(pairs):
                LH[i * part : (i + 1) * part, n * 4 * U : (n + 1) * 4 * U] = GB[p, here, :]

        def body(n, carry):
            cols = pl.ds(pl.multiple_of(n * nb_ig, nb_ig), nb_ig)
            total = lax.dot_general(
                LH[:, 0 : 4 * U], W[pairs[0], 0 : 4 * U, cols], NN, preferred_element_type=F32
            ) + lax.dot_general(
                LH[:, 4 * U :], W[pairs[1], 0 : 4 * U, cols], NN, preferred_element_type=F32
            )
            for i in range(4):
                term = total[i * part : (i + 1) * part]
                if pairs[0]:
                    term += IG[which, k0 + i // 2, i % 2, :, cols].astype(F32)
                IG[which, k0 + i // 2, i % 2, :, cols] = term.astype(BF16)
            return carry

        lax.fori_loop(0, feats // nb_ig, body, 0)

    def prob_terms():
        ones = jnp.ones((8, 2 * U), F32)
        for which in range(2):
            group = c if which == 0 else 1 - c
            for k in range(4):
                for h in range(2):
                    here = pl.ds(row_start(group, k, h), part)
                    PB[which, k, h, :, 0:part] = lax.dot_general(
                        ones, PT[here, :], NT, preferred_element_type=F32, precision=lax.Precision.HIGHEST
                    )

    locals_ = [
        pltpu.make_async_copy(ref, W.at[0, pl.ds(j * 2 * U, U), :], local_sem.at[j])
        for j, ref in enumerate((gate_hbm, up_hbm, down_hbm))
    ] + [
        pltpu.make_async_copy(x_hbm, X.at[mine, :], local_sem.at[3]),
        pltpu.make_async_copy(g_hbm, G.at[mine, :], local_sem.at[4]),
    ]
    gates = [
        pltpu.make_async_copy(prob_hbm, PV, local_sem.at[5]),
        pltpu.make_async_copy(count_hbm, count_ref, local_sem.at[6]),
    ]
    tasks = []

    def hand_on(needs, copy):
        @tasks.append
        def _():
            need(*needs)
            send(copy)

    def add_on(needs, ref, terms, copy):
        @tasks.append
        def _():
            need(*needs)
            add_to(ref, *terms)
            send(copy)

    both = (1, -1)
    arrivals = (
        [(GO_Z0, h) for h in CHUNKS],
        [(GO_L, e, h) for e in both for h in CHUNKS],
        [(GO_Z, e, h) for e in both for h in CHUNKS],
        [(k, h) for k in (GO_L2, GO_Z2) for h in CHUNKS],
    )
    for h in CHUNKS:
        t = TURN[h]
        hand_on((), (GO_Z0, h))
        for e in both:
            hand_on((), (GO_L, e, h))
            hand_on(((GO_L, e, h),), (GO_Z, e, h))
        hand_on(((GO_L, -t, h),), (GO_L2, h))
        hand_on(((GO_Z, -t, h) if h in ALONG_X else (GO_L2, h),), (GO_Z2, h))
        hand_on((), (BACK_Z0, h))
        hand_on((), (BACK_Z, -t, h))
        add_on(((BACK_Z, -t, h),), chunk(DG, l_at(-t), h), (RZ.at[1 + side(-t), h],), (BACK_L, -t, h)
        )
        if h in ALONG_X:
            hand_on((), (BACK_X2, h))
            hand_on((), (BACK_L2, h))
            add_on(((BACK_X2, h),), chunk(DG, z_at(t), h), (RZX.at[ALONG_X.index(h)],), (BACK_Z, t, h)
            )
        else:
            hand_on((), (BACK_Z, t, h))
            hand_on((), (BACK_Z2, h))
            add_on(((BACK_Z2, h),), chunk(DG, L2, h), (RZ.at[3, h],), (BACK_L2, h))
        add_on(((BACK_Z, t, h), (BACK_L2, h)), chunk(DG, l_at(t), h),
            (RZ.at[1 + side(t), h], RX2.at[h]), (BACK_L, t, h),
        )

        @tasks.append
        def _(h=h):
            need((BACK_Z0, h), (BACK_L, 1, h), (BACK_L, -1, h))
            out = (gate_out, up_out, down_out)[h // 2].at[pl.ds(h % 2 * half, half), :]
            add_into(out, chunk(DG, L0, h), RZ.at[0, h], RXF.at[0, h], RXF.at[1, h])

    @tasks.append
    def _():
        send(ROWS_X, ROWS_G)
        for copy in gates:
            copy.wait()
        for q in range(rows // 128):
            lines = pl.ds(pl.multiple_of(c * rows + q * 128, 128), 128)
            weights = jnp.broadcast_to(PV[q : q + 1, :], (128, 128)).T
            live = lax.broadcasted_iota(jnp.int32, (128, 128), 0) + q * 128 < count_ref[0]
            WC[lines, :] = jnp.where(live, weights, 0.0)
        send(ROWS_W)
        for copy in locals_:
            copy.wait()

    for p in range(4):
        for which in range(2):

            @tasks.append
            def _(p=p, which=which):
                need(*arrivals[p], *((ROWS_X, ROWS_G, ROWS_W) if which else ()))
                forward(p, which, (1 - c) * rows if which else c * rows)

        @tasks.append
        def _(p=p):
            weight_terms(p, 0, 4 * U, X)

        @tasks.append
        def _(p=p):
            weight_terms(p, 4 * U, 6 * U, G)

    for index in (1, 0):
        for k in (0, 2):
            for pairs in ((0, 1), (2, 3)):

                @tasks.append
                def _(index=index, k=k, pairs=pairs):
                    row_terms(index, 1 - c if index else c, k, pairs)

    @tasks.append
    def _():
        prob_terms()

    for k in range(4):

        @tasks.append
        def _(k=k):
            if k == 0:
                send((TWIN, PROB))
            send((TWIN, k))

        @tasks.append
        def _(k=k):
            if k == 0:
                need((TWIN, PROB))
                PB[0] = PB[0] + SIBP[...]
            need((TWIN, k))
            add_to(IG.at[0, k], SIB.at[k])

    for q in range(2):
        for k, h in ((0, 0), (0, 1), (1, 1), (2, 0)):

            @tasks.append
            def _(k=k, h=h, q=q):
                if q == 0:
                    send((ALONG_Y, k, h, PROB))
                send((ALONG_Y, k, h, q))

        for k, h in ((1, 0), (2, 1)):

            @tasks.append
            def _(k=k, h=h, q=q):
                if q == 0:
                    need((ALONG_Y, 0, h, PROB))
                    PB[0, k, h] = PB[0, k, h] + PR2[h]
                    send((ALONG_Y, k, h, PROB))
                need((ALONG_Y, 0, h, q))
                add_to(halves(IG.at[0, k, h])[q], halves(YR2.at[h])[q])
                send((ALONG_Y, k, h, q))

        @tasks.append
        def _(q=q):
            ends = ((1, 0), (1, 1), (2, 0), (2, 1))
            if q == 0:
                need(*((ALONG_Y, k, h, PROB) for k, h in ends))
                PB[0, 3] = PB[0, 3] + PF[0] + PF[1]
                send((FAR_Z, PROB))
            need(*((ALONG_Y, k, h, q) for k, h in ends))
            for h in range(2):
                add_to(halves(IG.at[0, 3, h])[q], halves(YF.at[0, h])[q], halves(YF.at[1, h])[q])
            send((FAR_Z, q))

    @tasks.append
    def _():
        need((FAR_Z, PROB), (FAR_Z, 0), (FAR_Z, 1))
        add_into(in_out, IG.at[0, 3, zh], ZF)
        lane = lax.broadcasted_iota(jnp.int32, (8, 128), 1)
        prob_out[...] = jnp.where(seq * part + lane < count_ref[0], PB[0, 3, zh] + PZ[...], 0.0)

    barrier = pltpu.get_barrier_semaphore()
    friends = (
        along_x(1), along_x(-1), along_y(1), along_y(-1), z_next, z_back, z_far, sibling,
    )
    for friend in friends:
        pl.semaphore_signal(barrier, inc=1, device_id=friend, device_id_type=MESH)
    for copy in gates + locals_:
        copy.start()
    PB[...] = jnp.zeros_like(PB)
    pl.semaphore_wait(barrier, len(friends))
    assert sorted(ORDER) == list(range(len(tasks)))
    for number in ORDER:
        tasks[number]()
    for copy in pending:
        copy.wait_send()


def finish(gate_in, up_in, down_in, rows_in, prob_in, gate_out, up_out, down_out, rows_out, prob_out, sems):
    pairs = ((gate_in, gate_out), (up_in, up_out), (down_in, down_out), (rows_in, rows_out))
    copies = [pltpu.make_async_copy(src, dst, sems.at[n]) for n, (src, dst) in enumerate(pairs)]
    for copy in copies:
        copy.start()
    prob_out[...] = prob_in[0, 0 : prob_out.shape[0]]
    for copy in copies:
        copy.wait()


N_SEMS = 113
VMEM_LIMIT = 61 << 20


def exchange(row_inputs, row_grads, gate_prob, live_counts, gate_t, up_t, down, blocks):
    rows, feats = row_inputs.shape
    units = down.shape[0]
    part = rows // 8
    any_space = pl.BlockSpec(memory_space=pl.ANY)
    piece = (units, feats)
    slab = (part, feats)
    tile = (8, 128)

    def held(*shape, kind=BF16):
        return pltpu.VMEM(shape, kind)

    return pl.pallas_call(
        functools.partial(kernel, units=units, rows=rows, feats=feats, blocks=blocks),
        out_shape=(
            held(*piece),
            held(*piece),
            held(*piece),
            held(*slab),
            held(*tile, kind=F32),
        ),
        in_specs=[any_space] * 7,
        out_specs=(pl.BlockSpec(memory_space=pltpu.VMEM),) * 5,
        scratch_shapes=[
            held(2 * rows, feats),
            held(2 * rows, feats),
            held(2 * rows, 128, kind=F32),
            held(4, 6 * units, feats),
            held(4, 2 * rows, 4 * units),
            held(6 * units, 2 * rows),
            held(2 * rows, 2 * units, kind=F32),
            held(4, 6 * units, feats),
            held(4, 6, units // 2, feats),
            held(len(ALONG_X), units // 2, feats),
            held(6, units // 2, feats),
            held(2, 6, units // 2, feats),
            held(2, 4, 2, *slab),
            held(4, 2, *slab),
            held(2, *slab),
            held(2, 2, *slab),
            held(*slab),
            held(4 * part, 8 * units),
            held(2, 4, 2, *tile, kind=F32),
            held(4, 2, *tile, kind=F32),
            held(2, *tile, kind=F32),
            held(2, 2, *tile, kind=F32),
            held(*tile, kind=F32),
            held(rows // 128, 128, kind=F32),
            pltpu.SMEM((1,), jnp.int32),
            pltpu.SemaphoreType.DMA((7,)),
            pltpu.SemaphoreType.DMA((N_SEMS,)),
            pltpu.SemaphoreType.DMA((N_SEMS,)),
        ],
        compiler_params=pltpu.CompilerParams(
            collective_id=0, has_side_effects=True, vmem_limit_bytes=VMEM_LIMIT
        ),
        cost_estimate=pl.CostEstimate(
            flops=16 * 2 * rows * 8 * units * feats, bytes_accessed=24 * rows * feats, transcendentals=16 * rows * units
        ),
        name="exchange",
    )(row_inputs, row_grads, gate_prob.reshape(-1, 128), live_counts, gate_t, up_t, down)


def hand_over(gate_t, up_t, down, rows_out, prob, part):
    any_space = pl.BlockSpec(memory_space=pl.ANY)
    vmem = pl.BlockSpec(memory_space=pltpu.VMEM)
    arrays = (gate_t, up_t, down, rows_out)
    return pl.pallas_call(
        finish,
        out_shape=tuple(jax.ShapeDtypeStruct(a.shape, a.dtype) for a in arrays)
        + (jax.ShapeDtypeStruct((part,), F32),),
        in_specs=[vmem] * 5,
        out_specs=(any_space,) * 4 + (vmem,),
        scratch_shapes=[pltpu.SemaphoreType.DMA((4,))],
        name="hand_over",
    )(*(pltpu.with_memory_space_constraint(a, pltpu.VMEM) for a in (*arrays, prob)))


def shards(blocks, row_inputs, row_grads, gate_prob, live_counts, gate_weight, up_weight, down_weight):
    results = exchange(
        row_inputs, row_grads, gate_prob, live_counts, gate_weight.T, up_weight.T, down_weight, blocks
    )
    gate_t, up_t, down_grad, input_grad, prob_grad = hand_over(*results, row_inputs.shape[0] // 8)
    return (input_grad, prob_grad, gate_t.T, up_t.T, down_grad)


def solution(mesh, blocks=(1024, 1024)):
    return jax.shard_map(
        functools.partial(shards, blocks),
        mesh=mesh,
        in_specs=(
            P("blk", None),
            P("blk", None),
            P("blk"),
            P("blk"),
            P(None, ("blk", "seq")),
            P(None, ("blk", "seq")),
            P(("blk", "seq"), None),
        ),
        out_specs=(
            P(("blk", "seq"), None),
            P(("blk", "seq")),
            P(None, ("blk", "seq")),
            P(None, ("blk", "seq")),
            P(("blk", "seq"), None),
        ),
        check_vma=False,
    )
```

```python
import functools

import jax
import jax.numpy as jnp
from jax import lax
from jax.experimental import pallas as pl
from jax.experimental.pallas import tpu as pltpu
from jax.sharding import PartitionSpec as P

MESH = pl.DeviceIdType.MESH
BF16 = jnp.bfloat16
F32 = jnp.float32
NT = (((1,), (1,)), ((), ()))
NN = (((1,), (0,)), ((), ()))

(
    GO_L, GO_Z0, GO_Z, GO_L2, GO_Z2, BACK_Z0, BACK_Z, BACK_Z2, BACK_X2, BACK_L2, BACK_L,
    ROWS_X, ROWS_G, ROWS_W, TWIN, ALONG_Y, FAR_Z, PROB,
) = range(18)

L0, Z0 = (0, 0), (0, 1)
L2, Z2 = (3, 0), (3, 1)
CHUNKS = range(6)
TURN = (1, 1, 1, -1, -1, -1)
GO_ALONG_X = (0, 1, 2, 3, 4, 5)
BACK_ALONG_X = (0, 5)
LAG = 60
ORDER = (
    18, 31, 75, 76, 63, 45, 90, 15, 61, 46, 16, 1, 0, 30, 32, 3, 60, 78, 19, 48, 33, 64, 4, 91, 47, 62, 21, 92, 5,
    79, 77, 65, 93, 49, 34, 96, 66, 2, 95, 98, 51, 6, 80, 109, 17, 97, 36, 111, 94, 82, 37, 20, 81, 22, 35, 100, 50,
    99, 102, 83, 101, 23, 38, 53, 25, 55, 107, 24, 8, 84, 103, 39, 104, 115, 54, 108, 105, 10, 116, 106, 86, 85, 26,
    112, 41, 117, 124, 132, 40, 56, 11, 118, 71, 110, 131, 70, 125, 9, 120, 113, 42, 114, 119, 27, 121, 57, 133,
    134, 68, 136, 135, 129, 122, 12, 52, 72, 43, 128, 126, 28, 87, 7, 58, 67, 73, 69, 127, 44, 123, 137, 59, 88, 13,
    130, 29, 74, 14, 139, 89, 138, 140,
)


def l_at(step):
    return (1, (1 - step) // 2)


def z_at(step):
    return (2, (1 - step) // 2)


def kernel(
    x_hbm, g_hbm, prob_hbm, count_hbm, gate_hbm, up_hbm, down_hbm,
    gate_out, up_out, down_out, in_out, prob_out,
    X, G, WC, W, GB, AT, PT, DG, RZ, RZX, RX2, RXF, IG, SIB, YR2, YF, ZF, LH,
    PB, SIBP, PR2, PF, PZ, PV, count_ref,
    local_sem, send_sem, recv_sem,
    *, units, rows, feats, blocks,
):
    U = units
    nb_dw, nb_ig = blocks
    part = rows // 8
    blk, seq = lax.axis_index("blk"), lax.axis_index("seq")
    c = lax.rem(blk, 2)
    x = lax.rem(blk // 2, 4)
    y = lax.rem(seq, 4)
    zh = seq // 4
    z = zh * 2 + blk // 8
    up = 1 - 2 * c

    def device(xx, yy, zz, cc):
        xx, yy, zz = lax.rem(xx + 8, 4), lax.rem(yy + 8, 4), lax.rem(zz + 8, 4)
        return ((lax.rem(zz, 2) * 4 + xx) * 2 + cc, (zz // 2) * 4 + yy)

    def along_x(step):
        return device(x + step, y, z, c)

    def along_y(step):
        return device(x, y + step, z, c)

    z_next, z_back, z_far = device(x, y, z + up, c), device(x, y, z - up, c), device(x, y, z + 2, c)
    sibling = device(x, y, z, 1 - c)
    half = U // 2

    def chunk(ref, slot, h):
        pair, place = slot
        return ref.at[pair, pl.ds(h // 2 * 2 * U + place * U + h % 2 * half, half), :]

    def side(step):
        return (1 - step) // 2

    routes = {}
    pending = []
    now = [0]
    here = set()

    def route(name, src, dst, target):
        number = len(routes)
        routes[name] = lambda: pltpu.make_async_remote_copy(
            src_ref=src, dst_ref=dst, send_sem=send_sem.at[number], recv_sem=recv_sem.at[number],
            device_id=target, device_id_type=MESH,
        )

    def send(*names):
        for name in names:
            copy = routes[name]()
            copy.start()
            pending.append((now[0], copy))

    def need(*names):
        for name in names:
            if name not in here:
                here.add(name)
                routes[name]().wait_recv()

    for h in CHUNKS:
        t = TURN[h]
        own = (gate_hbm, up_hbm, down_hbm)[h // 2].at[pl.ds(h % 2 * half, half), :]
        route((GO_Z0, h), own, chunk(W, Z0, h), z_next)
        route((BACK_Z0, h), chunk(DG, Z0, h), RZ.at[0, h], z_back)
        for e in (1, -1):
            route((GO_L, e, h), own, chunk(W, l_at(e), h), along_x(-e))
            route((GO_Z, e, h), chunk(W, l_at(e), h), chunk(W, z_at(e), h), z_next)
            route((BACK_Z, e, h), chunk(DG, z_at(e), h), RZ.at[1 + side(e), h], z_back)
            route((BACK_L, e, h), chunk(DG, l_at(e), h), RXF.at[side(e), h], along_x(e))
        route((GO_L2, h), chunk(W, l_at(-t), h), chunk(W, L2, h), along_x(t))
        route((BACK_L2, h), chunk(DG, L2, h), RX2.at[h], along_x(t))
        if h in GO_ALONG_X:
            route((GO_Z2, h), chunk(W, z_at(-t), h), chunk(W, Z2, h), along_x(t))
        else:
            route((GO_Z2, h), chunk(W, L2, h), chunk(W, Z2, h), z_next)
        if h in BACK_ALONG_X:
            route((BACK_X2, h), chunk(DG, Z2, h), RZX.at[BACK_ALONG_X.index(h)], along_x(t))
        else:
            route((BACK_Z2, h), chunk(DG, Z2, h), RZ.at[3, h], z_back)

    mine = pl.ds(pl.multiple_of(c * rows, rows), rows)
    route(ROWS_X, x_hbm, X.at[mine, :], sibling)
    route(ROWS_G, g_hbm, G.at[mine, :], sibling)
    route(ROWS_W, WC.at[mine, :], WC.at[mine, :], sibling)
    for k in range(4):
        route((TWIN, k), IG.at[1, k], SIB.at[k], sibling)
    route((TWIN, PROB), PB.at[1], SIBP, sibling)

    def halves(ref):
        return [ref.at[pl.ds(q * (part // 2), part // 2), :] for q in range(2)]

    for k, h in ((0, 0), (0, 1), (1, 0), (1, 1), (2, 0), (2, 1)):
        step = (1 if h == 0 else -1) if k == 0 else (1 if k == 1 else -1)
        dst, dst_p = (YR2.at[h], PR2.at[h]) if k == 0 else (YF.at[k - 1, h], PF.at[k - 1, h])
        for q, (a, b) in enumerate(zip(halves(IG.at[0, k, h]), halves(dst))):
            route((ALONG_Y, k, h, q), a, b, along_y(step))
        route((ALONG_Y, k, h, PROB), PB.at[0, k, h], dst_p, along_y(step))
    for q, (a, b) in enumerate(zip(halves(IG.at[0, 3, 1 - zh]), halves(ZF))):
        route((FAR_Z, q), a, b, z_far)
    route((FAR_Z, PROB), PB.at[0, 3, 1 - zh], PZ, z_far)
    assert len(routes) == send_sem.shape[0]

    def add_into(out, ref, *terms):
        total = ref[...].astype(F32)
        for term in terms:
            total += term[...].astype(F32)
        out[...] = total.astype(BF16)

    def add_to(ref, *terms):
        add_into(ref, ref, *terms)

    counted = set()

    def forward(p, which, first):
        lines = pl.ds(pl.multiple_of(first, rows), rows)
        pre = lax.dot_general(X[lines, :], W[p, 0 : 4 * U, :], NT, preferred_element_type=F32)
        back = lax.dot_general(G[lines, :], W[p, 4 * U : 6 * U, :], NT, preferred_element_type=F32)
        gate_pre, up_pre = pre[:, : 2 * U], pre[:, 2 * U :]
        s = jax.nn.sigmoid(gate_pre)
        activated = gate_pre * s
        hidden = activated * up_pre
        product = hidden.astype(BF16).astype(F32) * back
        if which in counted:
            PT[lines, :] += product
        else:
            PT[lines, :] = product
        counted.add(which)
        weight = WC[lines, :]
        weighted = weight * back
        gate_back = weighted * up_pre * s * (1.0 + gate_pre * (1.0 - s))
        up_back = weighted * activated
        GB[p, lines, 0 : 2 * U] = gate_back.astype(BF16)
        GB[p, lines, 2 * U :] = up_back.astype(BF16)
        AT[p, :, lines] = jnp.concatenate([gate_back, up_back, weight * hidden], axis=1).T.astype(BF16)

    def weight_terms(p, first, last, rows_ref):
        def body(i, carry):
            cols = pl.ds(pl.multiple_of(i * nb_dw, nb_dw), nb_dw)
            DG[p, first:last, cols] = lax.dot_general(
                AT[p, first:last, :], rows_ref[:, cols], NN, preferred_element_type=F32
            ).astype(BF16)
            return carry

        lax.fori_loop(0, feats // nb_dw, body, 0)

    steps_y = (2, 1, -1, 0)

    def row_start(group, k, h):
        return pl.multiple_of(group * rows + (h * 4 + lax.rem(y + steps_y[k] + 4, 4)) * part, part)

    def row_terms(which, group, k0, pairs):
        for i in range(4):
            here = pl.ds(row_start(group, k0 + i // 2, i % 2), part)
            for n, p in enumerate(pairs):
                LH[i * part : (i + 1) * part, n * 4 * U : (n + 1) * 4 * U] = GB[p, here, :]

        def body(n, carry):
            cols = pl.ds(pl.multiple_of(n * nb_ig, nb_ig), nb_ig)
            total = lax.dot_general(
                LH[:, 0 : 4 * U], W[pairs[0], 0 : 4 * U, cols], NN, preferred_element_type=F32
            ) + lax.dot_general(
                LH[:, 4 * U :], W[pairs[1], 0 : 4 * U, cols], NN, preferred_element_type=F32
            )
            for i in range(4):
                term = total[i * part : (i + 1) * part]
                if pairs[0]:
                    term += IG[which, k0 + i // 2, i % 2, :, cols].astype(F32)
                IG[which, k0 + i // 2, i % 2, :, cols] = term.astype(BF16)
            return carry

        lax.fori_loop(0, feats // nb_ig, body, 0)

    def prob_terms():
        ones = jnp.ones((8, 2 * U), F32)
        for which in range(2):
            group = c if which == 0 else 1 - c
            for k in range(4):
                for h in range(2):
                    here = pl.ds(row_start(group, k, h), part)
                    PB[which, k, h, :, 0:part] = lax.dot_general(
                        ones, PT[here, :], NT, preferred_element_type=F32, precision=lax.Precision.HIGHEST
                    )

    locals_ = [
        pltpu.make_async_copy(ref, W.at[0, pl.ds(j * 2 * U, U), :], local_sem.at[j])
        for j, ref in enumerate((gate_hbm, up_hbm, down_hbm))
    ] + [
        pltpu.make_async_copy(x_hbm, X.at[mine, :], local_sem.at[3]),
        pltpu.make_async_copy(g_hbm, G.at[mine, :], local_sem.at[4]),
    ]
    gates = [
        pltpu.make_async_copy(prob_hbm, PV, local_sem.at[5]),
        pltpu.make_async_copy(count_hbm, count_ref, local_sem.at[6]),
    ]
    tasks = []

    def hand_on(needs, copy):
        @tasks.append
        def _():
            need(*needs)
            send(copy)

    def add_on(needs, ref, terms, copy):
        @tasks.append
        def _():
            need(*needs)
            add_to(ref, *terms)
            send(copy)

    both = (1, -1)
    arrivals = (
        [(GO_Z0, h) for h in CHUNKS],
        [(GO_L, e, h) for e in both for h in CHUNKS],
        [(GO_Z, e, h) for e in both for h in CHUNKS],
        [(k, h) for k in (GO_L2, GO_Z2) for h in CHUNKS],
    )
    for h in CHUNKS:
        t = TURN[h]
        hand_on((), (GO_Z0, h))
        for e in both:
            hand_on((), (GO_L, e, h))
            hand_on(((GO_L, e, h),), (GO_Z, e, h))
        hand_on(((GO_L, -t, h),), (GO_L2, h))
        hand_on(((GO_Z, -t, h) if h in GO_ALONG_X else (GO_L2, h),), (GO_Z2, h))
        hand_on((), (BACK_Z0, h))
        hand_on((), (BACK_Z, -t, h))
        add_on(((BACK_Z, -t, h),), chunk(DG, l_at(-t), h), (RZ.at[1 + side(-t), h],), (BACK_L, -t, h)
        )
        if h in BACK_ALONG_X:
            hand_on((), (BACK_X2, h))
            hand_on((), (BACK_L2, h))
            add_on(((BACK_X2, h),), chunk(DG, z_at(t), h), (RZX.at[BACK_ALONG_X.index(h)],), (BACK_Z, t, h)
            )
        else:
            hand_on((), (BACK_Z, t, h))
            hand_on((), (BACK_Z2, h))
            add_on(((BACK_Z2, h),), chunk(DG, L2, h), (RZ.at[3, h],), (BACK_L2, h))
        add_on(((BACK_Z, t, h), (BACK_L2, h)), chunk(DG, l_at(t), h),
            (RZ.at[1 + side(t), h], RX2.at[h]), (BACK_L, t, h),
        )

        @tasks.append
        def _(h=h):
            need((BACK_Z0, h), (BACK_L, 1, h), (BACK_L, -1, h))
            out = (gate_out, up_out, down_out)[h // 2].at[pl.ds(h % 2 * half, half), :]
            add_into(out, chunk(DG, L0, h), RZ.at[0, h], RXF.at[0, h], RXF.at[1, h])

    @tasks.append
    def _():
        send(ROWS_X, ROWS_G)
        for copy in gates:
            copy.wait()
        for q in range(rows // 128):
            lines = pl.ds(pl.multiple_of(c * rows + q * 128, 128), 128)
            weights = jnp.broadcast_to(PV[q : q + 1, :], (128, 128)).T
            live = lax.broadcasted_iota(jnp.int32, (128, 128), 0) + q * 128 < count_ref[0]
            WC[lines, :] = jnp.where(live, weights, 0.0)
        send(ROWS_W)
        for copy in locals_:
            copy.wait()

    for p in range(4):
        for which in range(2):

            @tasks.append
            def _(p=p, which=which):
                need(*arrivals[p], *((ROWS_X, ROWS_G, ROWS_W) if which else ()))
                forward(p, which, (1 - c) * rows if which else c * rows)

        @tasks.append
        def _(p=p):
            weight_terms(p, 0, 4 * U, X)

        @tasks.append
        def _(p=p):
            weight_terms(p, 4 * U, 6 * U, G)

    for index in (1, 0):
        for k in (0, 2):
            for pairs in ((0, 1), (2, 3)):

                @tasks.append
                def _(index=index, k=k, pairs=pairs):
                    row_terms(index, 1 - c if index else c, k, pairs)

    @tasks.append
    def _():
        prob_terms()

    for k in range(4):

        @tasks.append
        def _(k=k):
            if k == 0:
                send((TWIN, PROB))
            send((TWIN, k))

        @tasks.append
        def _(k=k):
            if k == 0:
                need((TWIN, PROB))
                PB[0] = PB[0] + SIBP[...]
            need((TWIN, k))
            add_to(IG.at[0, k], SIB.at[k])

    for q in range(2):
        for k, h in ((0, 0), (0, 1), (1, 1), (2, 0)):

            @tasks.append
            def _(k=k, h=h, q=q):
                if q == 0:
                    send((ALONG_Y, k, h, PROB))
                send((ALONG_Y, k, h, q))

        for k, h in ((1, 0), (2, 1)):

            @tasks.append
            def _(k=k, h=h, q=q):
                if q == 0:
                    need((ALONG_Y, 0, h, PROB))
                    PB[0, k, h] = PB[0, k, h] + PR2[h]
                    send((ALONG_Y, k, h, PROB))
                need((ALONG_Y, 0, h, q))
                add_to(halves(IG.at[0, k, h])[q], halves(YR2.at[h])[q])
                send((ALONG_Y, k, h, q))

        @tasks.append
        def _(q=q):
            ends = ((1, 0), (1, 1), (2, 0), (2, 1))
            if q == 0:
                need(*((ALONG_Y, k, h, PROB) for k, h in ends))
                PB[0, 3] = PB[0, 3] + PF[0] + PF[1]
                send((FAR_Z, PROB))
            need(*((ALONG_Y, k, h, q) for k, h in ends))
            for h in range(2):
                add_to(halves(IG.at[0, 3, h])[q], halves(YF.at[0, h])[q], halves(YF.at[1, h])[q])
            send((FAR_Z, q))

    for q in range(2):

        @tasks.append
        def _(q=q):
            need((FAR_Z, q))
            add_into(halves(in_out)[q], halves(IG.at[0, 3, zh])[q], halves(ZF)[q])

    @tasks.append
    def _():
        need((FAR_Z, PROB))
        lane = lax.broadcasted_iota(jnp.int32, (8, 128), 1)
        prob_out[...] = jnp.where(seq * part + lane < count_ref[0], PB[0, 3, zh] + PZ[...], 0.0)

    barrier = pltpu.get_barrier_semaphore()
    friends = (
        along_x(1), along_x(-1), along_y(1), along_y(-1), z_next, z_back, z_far, sibling,
    )
    for friend in friends:
        pl.semaphore_signal(barrier, inc=1, device_id=friend, device_id_type=MESH)
    for copy in gates + locals_:
        copy.start()
    PB[...] = jnp.zeros_like(PB)
    pl.semaphore_wait(barrier, len(friends))
    assert sorted(ORDER) == list(range(len(tasks)))
    for place, number in enumerate(ORDER):
        now[0] = place
        tasks[number]()
        while pending and pending[0][0] < place - LAG:
            pending.pop(0)[1].wait_send()
    for _, copy in pending:
        copy.wait_send()


def finish(gate_in, up_in, down_in, rows_in, prob_in, gate_out, up_out, down_out, rows_out, prob_out, sems):
    pairs = ((gate_in, gate_out), (up_in, up_out), (down_in, down_out), (rows_in, rows_out))
    copies = [pltpu.make_async_copy(src, dst, sems.at[n]) for n, (src, dst) in enumerate(pairs)]
    for copy in copies:
        copy.start()
    prob_out[...] = prob_in[0, 0 : prob_out.shape[0]]
    for copy in copies:
        copy.wait()


N_SEMS = 113
VMEM_LIMIT = 61 << 20


def exchange(row_inputs, row_grads, gate_prob, live_counts, gate_t, up_t, down, blocks):
    rows, feats = row_inputs.shape
    units = down.shape[0]
    part = rows // 8
    any_space = pl.BlockSpec(memory_space=pl.ANY)
    piece = (units, feats)
    slab = (part, feats)
    tile = (8, 128)

    def held(*shape, kind=BF16):
        return pltpu.VMEM(shape, kind)

    return pl.pallas_call(
        functools.partial(kernel, units=units, rows=rows, feats=feats, blocks=blocks),
        out_shape=(
            held(*piece),
            held(*piece),
            held(*piece),
            held(*slab),
            held(*tile, kind=F32),
        ),
        in_specs=[any_space] * 7,
        out_specs=(pl.BlockSpec(memory_space=pltpu.VMEM),) * 5,
        scratch_shapes=[
            held(2 * rows, feats),
            held(2 * rows, feats),
            held(2 * rows, 128, kind=F32),
            held(4, 6 * units, feats),
            held(4, 2 * rows, 4 * units),
            held(4, 6 * units, 2 * rows),
            held(2 * rows, 2 * units, kind=F32),
            held(4, 6 * units, feats),
            held(4, 6, units // 2, feats),
            held(len(BACK_ALONG_X), units // 2, feats),
            held(6, units // 2, feats),
            held(2, 6, units // 2, feats),
            held(2, 4, 2, *slab),
            held(4, 2, *slab),
            held(2, *slab),
            held(2, 2, *slab),
            held(*slab),
            held(4 * part, 8 * units),
            held(2, 4, 2, *tile, kind=F32),
            held(4, 2, *tile, kind=F32),
            held(2, *tile, kind=F32),
            held(2, 2, *tile, kind=F32),
            held(*tile, kind=F32),
            held(rows // 128, 128, kind=F32),
            pltpu.SMEM((1,), jnp.int32),
            pltpu.SemaphoreType.DMA((7,)),
            pltpu.SemaphoreType.DMA((N_SEMS,)),
            pltpu.SemaphoreType.DMA((N_SEMS,)),
        ],
        compiler_params=pltpu.CompilerParams(
            collective_id=0, has_side_effects=True, vmem_limit_bytes=VMEM_LIMIT
        ),
        cost_estimate=pl.CostEstimate(
            flops=16 * 2 * rows * 8 * units * feats, bytes_accessed=24 * rows * feats, transcendentals=16 * rows * units
        ),
        name="exchange",
    )(row_inputs, row_grads, gate_prob.reshape(-1, 128), live_counts, gate_t, up_t, down)


def hand_over(gate_t, up_t, down, rows_out, prob, part):
    any_space = pl.BlockSpec(memory_space=pl.ANY)
    vmem = pl.BlockSpec(memory_space=pltpu.VMEM)
    arrays = (gate_t, up_t, down, rows_out)
    return pl.pallas_call(
        finish,
        out_shape=tuple(jax.ShapeDtypeStruct(a.shape, a.dtype) for a in arrays)
        + (jax.ShapeDtypeStruct((part,), F32),),
        in_specs=[vmem] * 5,
        out_specs=(any_space,) * 4 + (vmem,),
        scratch_shapes=[pltpu.SemaphoreType.DMA((4,))],
        name="hand_over",
    )(*(pltpu.with_memory_space_constraint(a, pltpu.VMEM) for a in (*arrays, prob)))


def shards(blocks, row_inputs, row_grads, gate_prob, live_counts, gate_weight, up_weight, down_weight):
    results = exchange(
        row_inputs, row_grads, gate_prob, live_counts, gate_weight.T, up_weight.T, down_weight, blocks
    )
    gate_t, up_t, down_grad, input_grad, prob_grad = hand_over(*results, row_inputs.shape[0] // 8)
    return (input_grad, prob_grad, gate_t.T, up_t.T, down_grad)


def solution(mesh, blocks=(1024, 1024)):
    return jax.shard_map(
        functools.partial(shards, blocks),
        mesh=mesh,
        in_specs=(
            P("blk", None),
            P("blk", None),
            P("blk"),
            P("blk"),
            P(None, ("blk", "seq")),
            P(None, ("blk", "seq")),
            P(("blk", "seq"), None),
        ),
        out_specs=(
            P(("blk", "seq"), None),
            P(("blk", "seq")),
            P(None, ("blk", "seq")),
            P(None, ("blk", "seq")),
            P(("blk", "seq"), None),
        ),
        check_vma=False,
    )
```

```python
import functools

import jax
import jax.numpy as jnp
from jax import lax
from jax.experimental import pallas as pl
from jax.experimental.pallas import tpu as pltpu
from jax.sharding import PartitionSpec as P

MESH = pl.DeviceIdType.MESH
BF16 = jnp.bfloat16
F32 = jnp.float32
NT = (((1,), (1,)), ((), ()))
NN = (((1,), (0,)), ((), ()))

(
    GO_L, GO_Z0, GO_Z, GO_L2, GO_Z2, BACK_Z0, BACK_Z, BACK_Z2, BACK_X2, BACK_L2, BACK_L,
    ROWS_X, ROWS_G, ROWS_W, TWIN, ALONG_Y, FAR_Z, PROB,
) = range(18)

L0, Z0 = (0, 0), (0, 1)
L2, Z2 = (3, 0), (3, 1)
CHUNKS = range(6)
TURN = (1, 1, 1, -1, -1, -1)
GO_ALONG_X = (0, 1, 2, 3, 4, 5)
BACK_ALONG_X = (0, 5)
LAG = 60
ORDER = (
    18, 31, 75, 76, 63, 45, 90, 15, 61, 46, 16, 1, 0, 30, 32, 3, 60, 78, 19, 48, 33, 64, 4, 91, 47, 62, 21, 92, 5,
    79, 77, 65, 93, 49, 34, 96, 66, 2, 95, 98, 51, 6, 80, 109, 17, 97, 36, 111, 94, 82, 37, 20, 81, 22, 35, 100, 50,
    99, 102, 83, 101, 23, 38, 53, 25, 55, 107, 24, 8, 84, 103, 39, 104, 115, 54, 108, 105, 10, 116, 106, 86, 85, 26,
    112, 41, 117, 124, 132, 40, 56, 11, 118, 71, 110, 131, 70, 125, 9, 120, 113, 42, 114, 119, 27, 121, 57, 133,
    134, 68, 136, 135, 129, 122, 12, 52, 72, 43, 128, 126, 28, 87, 7, 58, 67, 73, 69, 127, 44, 123, 137, 59, 88, 13,
    130, 29, 74, 14, 139, 89, 138, 140,
)


def l_at(step):
    return (1, (1 - step) // 2)


def z_at(step):
    return (2, (1 - step) // 2)


def kernel(
    x_hbm, g_hbm, prob_hbm, count_hbm, gate_hbm, up_hbm, down_hbm,
    gate_out, up_out, down_out, in_out, prob_out,
    X, G, WC, W, GB, AT, PT, DG, RZ, RZX, RX2, RXF, IG, SIB, YR2, YF, ZF, LH,
    PB, SIBP, PR2, PF, PZ, PV, count_ref,
    local_sem, send_sem, recv_sem,
    *, units, rows, feats, blocks,
):
    U = units
    nb_dw, nb_ig = blocks
    part = rows // 8
    blk, seq = lax.axis_index("blk"), lax.axis_index("seq")
    c = lax.rem(blk, 2)
    x = lax.rem(blk // 2, 4)
    y = lax.rem(seq, 4)
    zh = seq // 4
    z = zh * 2 + blk // 8
    up = 1 - 2 * c

    def device(xx, yy, zz, cc):
        xx, yy, zz = lax.rem(xx + 8, 4), lax.rem(yy + 8, 4), lax.rem(zz + 8, 4)
        return ((lax.rem(zz, 2) * 4 + xx) * 2 + cc, (zz // 2) * 4 + yy)

    def along_x(step):
        return device(x + step, y, z, c)

    def along_y(step):
        return device(x, y + step, z, c)

    z_next, z_back, z_far = device(x, y, z + up, c), device(x, y, z - up, c), device(x, y, z + 2, c)
    sibling = device(x, y, z, 1 - c)
    half = U // 2

    def chunk(ref, slot, h):
        pair, place = slot
        return ref.at[pair, pl.ds(h // 2 * 2 * U + place * U + h % 2 * half, half), :]

    def side(step):
        return (1 - step) // 2

    routes = {}
    pending = []
    now = [0]
    here = set()

    def route(name, src, dst, target):
        number = len(routes)
        routes[name] = lambda: pltpu.make_async_remote_copy(
            src_ref=src, dst_ref=dst, send_sem=send_sem.at[number], recv_sem=recv_sem.at[number],
            device_id=target, device_id_type=MESH,
        )

    def send(*names):
        for name in names:
            copy = routes[name]()
            copy.start()
            pending.append((now[0], copy))

    def need(*names):
        for name in names:
            if name not in here:
                here.add(name)
                routes[name]().wait_recv()

    for h in CHUNKS:
        t = TURN[h]
        own = (gate_hbm, up_hbm, down_hbm)[h // 2].at[pl.ds(h % 2 * half, half), :]
        route((GO_Z0, h), own, chunk(W, Z0, h), z_next)
        route((BACK_Z0, h), chunk(DG, Z0, h), RZ.at[0, h], z_back)
        for e in (1, -1):
            route((GO_L, e, h), own, chunk(W, l_at(e), h), along_x(-e))
            route((GO_Z, e, h), chunk(W, l_at(e), h), chunk(W, z_at(e), h), z_next)
            route((BACK_Z, e, h), chunk(DG, z_at(e), h), RZ.at[1 + side(e), h], z_back)
            route((BACK_L, e, h), chunk(DG, l_at(e), h), RXF.at[side(e), h], along_x(e))
        route((GO_L2, h), chunk(W, l_at(-t), h), chunk(W, L2, h), along_x(t))
        route((BACK_L2, h), chunk(DG, L2, h), RX2.at[h], along_x(t))
        if h in GO_ALONG_X:
            route((GO_Z2, h), chunk(W, z_at(-t), h), chunk(W, Z2, h), along_x(t))
        else:
            route((GO_Z2, h), chunk(W, L2, h), chunk(W, Z2, h), z_next)
        if h in BACK_ALONG_X:
            route((BACK_X2, h), chunk(DG, Z2, h), RZX.at[BACK_ALONG_X.index(h)], along_x(t))
        else:
            route((BACK_Z2, h), chunk(DG, Z2, h), RZ.at[3, h], z_back)

    mine = pl.ds(pl.multiple_of(c * rows, rows), rows)
    route(ROWS_X, x_hbm, X.at[mine, :], sibling)
    route(ROWS_G, g_hbm, G.at[mine, :], sibling)
    route(ROWS_W, WC.at[mine, :], WC.at[mine, :], sibling)
    for k in range(4):
        route((TWIN, k), IG.at[1, k], SIB.at[k], sibling)
    route((TWIN, PROB), PB.at[1], SIBP, sibling)

    def halves(ref):
        return [ref.at[pl.ds(q * (part // 2), part // 2), :] for q in range(2)]

    for k, h in ((0, 0), (0, 1), (1, 0), (1, 1), (2, 0), (2, 1)):
        step = (1 if h == 0 else -1) if k == 0 else (1 if k == 1 else -1)
        dst, dst_p = (YR2.at[h], PR2.at[h]) if k == 0 else (YF.at[k - 1, h], PF.at[k - 1, h])
        for q, (a, b) in enumerate(zip(halves(IG.at[0, k, h]), halves(dst))):
            route((ALONG_Y, k, h, q), a, b, along_y(step))
        route((ALONG_Y, k, h, PROB), PB.at[0, k, h], dst_p, along_y(step))
    for q, (a, b) in enumerate(zip(halves(IG.at[0, 3, 1 - zh]), halves(ZF))):
        route((FAR_Z, q), a, b, z_far)
    route((FAR_Z, PROB), PB.at[0, 3, 1 - zh], PZ, z_far)
    assert len(routes) == send_sem.shape[0]

    def add_into(out, ref, *terms):
        total = ref[...].astype(F32)
        for term in terms:
            total += term[...].astype(F32)
        out[...] = total.astype(BF16)

    def add_to(ref, *terms):
        add_into(ref, ref, *terms)

    counted = set()

    def forward(p, which, first):
        lines = pl.ds(pl.multiple_of(first, rows), rows)
        pre = lax.dot_general(X[lines, :], W[p, 0 : 4 * U, :], NT, preferred_element_type=F32)
        back = lax.dot_general(G[lines, :], W[p, 4 * U : 6 * U, :], NT, preferred_element_type=F32)
        gate_pre, up_pre = pre[:, : 2 * U], pre[:, 2 * U :]
        s = jax.nn.sigmoid(gate_pre)
        activated = gate_pre * s
        hidden = activated * up_pre
        product = hidden.astype(BF16).astype(F32) * back
        if which in counted:
            PT[lines, :] += product
        else:
            PT[lines, :] = product
        counted.add(which)
        weight = WC[lines, :]
        weighted = weight * back
        gate_back = weighted * up_pre * s * (1.0 + gate_pre * (1.0 - s))
        up_back = weighted * activated
        GB[p, lines, 0 : 2 * U] = gate_back.astype(BF16)
        GB[p, lines, 2 * U :] = up_back.astype(BF16)
        AT[p, :, lines] = jnp.concatenate([gate_back, up_back, weight * hidden], axis=1).T.astype(BF16)

    def weight_terms(p, first, last, rows_ref):
        def body(i, carry):
            cols = pl.ds(pl.multiple_of(i * nb_dw, nb_dw), nb_dw)
            DG[p, first:last, cols] = lax.dot_general(
                AT[p, first:last, :], rows_ref[:, cols], NN, preferred_element_type=F32
            ).astype(BF16)
            return carry

        lax.fori_loop(0, feats // nb_dw, body, 0)

    steps_y = (2, 1, -1, 0)

    def row_start(group, k, h):
        return pl.multiple_of(group * rows + (h * 4 + lax.rem(y + steps_y[k] + 4, 4)) * part, part)

    def row_terms(which, group, k0, pairs):
        for i in range(4):
            here = pl.ds(row_start(group, k0 + i // 2, i % 2), part)
            for n, p in enumerate(pairs):
                LH[i * part : (i + 1) * part, n * 4 * U : (n + 1) * 4 * U] = GB[p, here, :]

        def body(n, carry):
            cols = pl.ds(pl.multiple_of(n * nb_ig, nb_ig), nb_ig)
            total = lax.dot_general(
                LH[:, 0 : 4 * U], W[pairs[0], 0 : 4 * U, cols], NN, preferred_element_type=F32
            ) + lax.dot_general(
                LH[:, 4 * U :], W[pairs[1], 0 : 4 * U, cols], NN, preferred_element_type=F32
            )
            for i in range(4):
                term = total[i * part : (i + 1) * part]
                if pairs[0]:
                    term += IG[which, k0 + i // 2, i % 2, :, cols].astype(F32)
                IG[which, k0 + i // 2, i % 2, :, cols] = term.astype(BF16)
            return carry

        lax.fori_loop(0, feats // nb_ig, body, 0)

    def prob_terms():
        ones = jnp.ones((8, 2 * U), F32)
        for which in range(2):
            group = c if which == 0 else 1 - c
            for k in range(4):
                for h in range(2):
                    here = pl.ds(row_start(group, k, h), part)
                    PB[which, k, h, :, 0:part] = lax.dot_general(
                        ones, PT[here, :], NT, preferred_element_type=F32, precision=lax.Precision.HIGHEST
                    )

    locals_ = [
        pltpu.make_async_copy(ref, W.at[0, pl.ds(j * 2 * U, U), :], local_sem.at[j])
        for j, ref in enumerate((gate_hbm, up_hbm, down_hbm))
    ] + [
        pltpu.make_async_copy(x_hbm, X.at[mine, :], local_sem.at[3]),
        pltpu.make_async_copy(g_hbm, G.at[mine, :], local_sem.at[4]),
    ]
    gates = [
        pltpu.make_async_copy(prob_hbm, PV, local_sem.at[5]),
        pltpu.make_async_copy(count_hbm, count_ref, local_sem.at[6]),
    ]
    tasks = []

    def hand_on(needs, copy):
        @tasks.append
        def _():
            need(*needs)
            send(copy)

    def add_on(needs, ref, terms, copy):
        @tasks.append
        def _():
            need(*needs)
            add_to(ref, *terms)
            send(copy)

    both = (1, -1)
    arrivals = (
        [(GO_Z0, h) for h in CHUNKS],
        [(GO_L, e, h) for e in both for h in CHUNKS],
        [(GO_Z, e, h) for e in both for h in CHUNKS],
        [(k, h) for k in (GO_L2, GO_Z2) for h in CHUNKS],
    )
    for h in CHUNKS:
        t = TURN[h]
        hand_on((), (GO_Z0, h))
        for e in both:
            hand_on((), (GO_L, e, h))
            hand_on(((GO_L, e, h),), (GO_Z, e, h))
        hand_on(((GO_L, -t, h),), (GO_L2, h))
        hand_on(((GO_Z, -t, h) if h in GO_ALONG_X else (GO_L2, h),), (GO_Z2, h))
        hand_on((), (BACK_Z0, h))
        hand_on((), (BACK_Z, -t, h))
        add_on(((BACK_Z, -t, h),), chunk(DG, l_at(-t), h), (RZ.at[1 + side(-t), h],), (BACK_L, -t, h)
        )
        if h in BACK_ALONG_X:
            hand_on((), (BACK_X2, h))
            hand_on((), (BACK_L2, h))
            add_on(((BACK_X2, h),), chunk(DG, z_at(t), h), (RZX.at[BACK_ALONG_X.index(h)],), (BACK_Z, t, h)
            )
        else:
            hand_on((), (BACK_Z, t, h))
            hand_on((), (BACK_Z2, h))
            add_on(((BACK_Z2, h),), chunk(DG, L2, h), (RZ.at[3, h],), (BACK_L2, h))
        add_on(((BACK_Z, t, h), (BACK_L2, h)), chunk(DG, l_at(t), h),
            (RZ.at[1 + side(t), h], RX2.at[h]), (BACK_L, t, h),
        )

        @tasks.append
        def _(h=h):
            need((BACK_Z0, h), (BACK_L, 1, h), (BACK_L, -1, h))
            out = (gate_out, up_out, down_out)[h // 2].at[pl.ds(h % 2 * half, half), :]
            add_into(out, chunk(DG, L0, h), RZ.at[0, h], RXF.at[0, h], RXF.at[1, h])

    @tasks.append
    def _():
        send(ROWS_X, ROWS_G)
        for copy in gates:
            copy.wait()
        for q in range(rows // 128):
            lines = pl.ds(pl.multiple_of(c * rows + q * 128, 128), 128)
            weights = jnp.broadcast_to(PV[q : q + 1, :], (128, 128)).T
            live = lax.broadcasted_iota(jnp.int32, (128, 128), 0) + q * 128 < count_ref[0]
            WC[lines, :] = jnp.where(live, weights, 0.0)
        send(ROWS_W)
        for copy in locals_:
            copy.wait()

    for p in range(4):
        for which in range(2):

            @tasks.append
            def _(p=p, which=which):
                need(*arrivals[p], *((ROWS_X, ROWS_G, ROWS_W) if which else ()))
                forward(p, which, (1 - c) * rows if which else c * rows)

        @tasks.append
        def _(p=p):
            weight_terms(p, 0, 4 * U, X)

        @tasks.append
        def _(p=p):
            weight_terms(p, 4 * U, 6 * U, G)

    for index in (1, 0):
        for k in (0, 2):
            for pairs in ((0, 1), (2, 3)):

                @tasks.append
                def _(index=index, k=k, pairs=pairs):
                    row_terms(index, 1 - c if index else c, k, pairs)

    @tasks.append
    def _():
        prob_terms()

    for k in range(4):

        @tasks.append
        def _(k=k):
            if k == 0:
                send((TWIN, PROB))
            send((TWIN, k))

        @tasks.append
        def _(k=k):
            if k == 0:
                need((TWIN, PROB))
                PB[0] = PB[0] + SIBP[...]
            need((TWIN, k))
            add_to(IG.at[0, k], SIB.at[k])

    for q in range(2):
        for k, h in ((0, 0), (0, 1), (1, 1), (2, 0)):

            @tasks.append
            def _(k=k, h=h, q=q):
                if q == 0:
                    send((ALONG_Y, k, h, PROB))
                send((ALONG_Y, k, h, q))

        for k, h in ((1, 0), (2, 1)):

            @tasks.append
            def _(k=k, h=h, q=q):
                if q == 0:
                    need((ALONG_Y, 0, h, PROB))
                    PB[0, k, h] = PB[0, k, h] + PR2[h]
                    send((ALONG_Y, k, h, PROB))
                need((ALONG_Y, 0, h, q))
                add_to(halves(IG.at[0, k, h])[q], halves(YR2.at[h])[q])
                send((ALONG_Y, k, h, q))

        @tasks.append
        def _(q=q):
            ends = ((1, 0), (1, 1), (2, 0), (2, 1))
            if q == 0:
                need(*((ALONG_Y, k, h, PROB) for k, h in ends))
                PB[0, 3] = PB[0, 3] + PF[0] + PF[1]
                send((FAR_Z, PROB))
            need(*((ALONG_Y, k, h, q) for k, h in ends))
            for h in range(2):
                add_to(halves(IG.at[0, 3, h])[q], halves(YF.at[0, h])[q], halves(YF.at[1, h])[q])
            send((FAR_Z, q))

    for q in range(2):

        @tasks.append
        def _(q=q):
            need((FAR_Z, q))
            add_into(halves(in_out)[q], halves(IG.at[0, 3, zh])[q], halves(ZF)[q])

    @tasks.append
    def _():
        need((FAR_Z, PROB))
        lane = lax.broadcasted_iota(jnp.int32, (8, 128), 1)
        prob_out[...] = jnp.where(seq * part + lane < count_ref[0], PB[0, 3, zh] + PZ[...], 0.0)

    barrier = pltpu.get_barrier_semaphore()
    friends = (
        along_x(1), along_x(-1), along_y(1), along_y(-1), z_next, z_back, z_far, sibling,
    )
    for friend in friends:
        pl.semaphore_signal(barrier, inc=1, device_id=friend, device_id_type=MESH)
    for copy in gates + locals_:
        copy.start()
    PB[...] = jnp.zeros_like(PB)
    pl.semaphore_wait(barrier, len(friends))
    assert sorted(ORDER) == list(range(len(tasks)))
    for place, number in enumerate(ORDER):
        now[0] = place
        tasks[number]()
        while pending and pending[0][0] < place - LAG:
            pending.pop(0)[1].wait_send()
    for _, copy in pending:
        copy.wait_send()


def finish(gate_in, up_in, down_in, rows_in, prob_in, gate_out, up_out, down_out, rows_out, prob_out, sems):
    pairs = ((gate_in, gate_out), (up_in, up_out), (down_in, down_out), (rows_in, rows_out))
    half = gate_in.shape[0] // 2
    copies = [
        pltpu.make_async_copy(src.at[pl.ds(q * half, half), :], dst.at[pl.ds(q * half, half), :], sems.at[2 * n + q])
        for n, (src, dst) in enumerate(pairs)
        for q in range(2)
    ]
    for copy in copies:
        copy.start()
    prob_out[...] = prob_in[0, 0 : prob_out.shape[0]]
    for copy in copies:
        copy.wait()


N_SEMS = 113
VMEM_LIMIT = 61 << 20


def exchange(row_inputs, row_grads, gate_prob, live_counts, gate_t, up_t, down, blocks):
    rows, feats = row_inputs.shape
    units = down.shape[0]
    part = rows // 8
    any_space = pl.BlockSpec(memory_space=pl.ANY)
    piece = (units, feats)
    slab = (part, feats)
    tile = (8, 128)

    def held(*shape, kind=BF16):
        return pltpu.VMEM(shape, kind)

    return pl.pallas_call(
        functools.partial(kernel, units=units, rows=rows, feats=feats, blocks=blocks),
        out_shape=(
            held(*piece),
            held(*piece),
            held(*piece),
            held(*slab),
            held(*tile, kind=F32),
        ),
        in_specs=[any_space] * 7,
        out_specs=(pl.BlockSpec(memory_space=pltpu.VMEM),) * 5,
        scratch_shapes=[
            held(2 * rows, feats),
            held(2 * rows, feats),
            held(2 * rows, 128, kind=F32),
            held(4, 6 * units, feats),
            held(4, 2 * rows, 4 * units),
            held(4, 6 * units, 2 * rows),
            held(2 * rows, 2 * units, kind=F32),
            held(4, 6 * units, feats),
            held(4, 6, units // 2, feats),
            held(len(BACK_ALONG_X), units // 2, feats),
            held(6, units // 2, feats),
            held(2, 6, units // 2, feats),
            held(2, 4, 2, *slab),
            held(4, 2, *slab),
            held(2, *slab),
            held(2, 2, *slab),
            held(*slab),
            held(4 * part, 8 * units),
            held(2, 4, 2, *tile, kind=F32),
            held(4, 2, *tile, kind=F32),
            held(2, *tile, kind=F32),
            held(2, 2, *tile, kind=F32),
            held(*tile, kind=F32),
            held(rows // 128, 128, kind=F32),
            pltpu.SMEM((1,), jnp.int32),
            pltpu.SemaphoreType.DMA((7,)),
            pltpu.SemaphoreType.DMA((N_SEMS,)),
            pltpu.SemaphoreType.DMA((N_SEMS,)),
        ],
        compiler_params=pltpu.CompilerParams(
            collective_id=0, has_side_effects=True, vmem_limit_bytes=VMEM_LIMIT
        ),
        cost_estimate=pl.CostEstimate(
            flops=16 * 2 * rows * 8 * units * feats, bytes_accessed=24 * rows * feats, transcendentals=16 * rows * units
        ),
        name="exchange",
    )(row_inputs, row_grads, gate_prob.reshape(-1, 128), live_counts, gate_t, up_t, down)


def hand_over(gate_t, up_t, down, rows_out, prob, part):
    any_space = pl.BlockSpec(memory_space=pl.ANY)
    vmem = pl.BlockSpec(memory_space=pltpu.VMEM)
    arrays = (gate_t, up_t, down, rows_out)
    return pl.pallas_call(
        finish,
        out_shape=tuple(jax.ShapeDtypeStruct(a.shape, a.dtype) for a in arrays)
        + (jax.ShapeDtypeStruct((part,), F32),),
        in_specs=[vmem] * 5,
        out_specs=(any_space,) * 4 + (vmem,),
        scratch_shapes=[pltpu.SemaphoreType.DMA((8,))],
        name="hand_over",
    )(*(pltpu.with_memory_space_constraint(a, pltpu.VMEM) for a in (*arrays, prob)))


def shards(blocks, row_inputs, row_grads, gate_prob, live_counts, gate_weight, up_weight, down_weight):
    results = exchange(
        row_inputs, row_grads, gate_prob, live_counts, gate_weight.T, up_weight.T, down_weight, blocks
    )
    gate_t, up_t, down_grad, input_grad, prob_grad = hand_over(*results, row_inputs.shape[0] // 8)
    return (input_grad, prob_grad, gate_t.T, up_t.T, down_grad)


def solution(mesh, blocks=(1024, 1024)):
    return jax.shard_map(
        functools.partial(shards, blocks),
        mesh=mesh,
        in_specs=(
            P("blk", None),
            P("blk", None),
            P("blk"),
            P("blk"),
            P(None, ("blk", "seq")),
            P(None, ("blk", "seq")),
            P(("blk", "seq"), None),
        ),
        out_specs=(
            P(("blk", "seq"), None),
            P(("blk", "seq")),
            P(None, ("blk", "seq")),
            P(None, ("blk", "seq")),
            P(("blk", "seq"), None),
        ),
        check_vma=False,
    )
```
